256 devices in a mesh: snap: 2 (over z_hi), row: 8 (over z_lo, core), col: 16 (over x, y).
Axes of the slice: x: 4, y: 4, z: 8 (z_hi: 2, z_lo: 4; z = z_hi * 4 + z_lo), core: 2. Of those that a mesh axis runs over, the one named last changes fastest.
Arguments:
- states: float32 [4096, 240], P(('snap', 'row', 'col')), may hold values from -8 to 8, as said below
- derivatives: float32 [4096, 240], P(('snap', 'row', 'col')), may hold values from -6 to 6
- tile_map: int32 [2048, 2], P(('snap', 'row', 'col')), may hold values from -1 to 113, as said below
Outputs:
- gram_tiles: float32 [2048, 256, 256], P(('snap', 'row', 'col'))
- rhs_blocks: float32 [128, 256, 240], P(('row', 'col'), None, 'snap')
The draws below stay inside these ranges and needn't reach their ends.
Inputs may be any that keep to these rules, and one draw needn't show every extreme that they name: `states`: states are real coordinates of snapshots. `tile_map`: each entry is a pair a <= b of column tiles, or (-1, -1) for an empty slot; no pair appears twice. Each device's 8 slots hold its live pairs first, then empty ones; each device has at least 2 live slots and some device has all 8 live.
All inputs are finite; a program needn't handle non-finite values.
Results may differ from the reference program's by a relative error of at most 0.0003.
Values sent between devices are 32-bit elements; how exact they have to be, the bound alone decides.
A program may use at most 128 MiB of HBM per device.

```python
import jax
import jax.numpy as jnp
import numpy as np
from jax import lax

R = 240
TW = 256
CTILES = 114
SNAPS = 4096
SLOT_DEV = 8
SLOTS = 2048
N_ROW = 8
N_COL = 16


def draw_states(key, part):
    key = jax.random.fold_in(key, 5)
    key_scale, key_body = jax.random.split(key)
    column_scales = jnp.exp(jax.random.uniform(key_scale, (1, R), minval=jnp.log(0.25), maxval=jnp.log(1.5)))
    samples = jax.random.normal(key_body, (SNAPS, R))
    return jnp.clip(samples * column_scales, -8.0, 8.0).astype(jnp.float32)


def draw_tile_map(key, part):
    key = jax.random.fold_in(key, 11)
    key_order, key_live, key_full = jax.random.split(key, 3)
    upper_rows, upper_cols = np.triu_indices(CTILES)
    total_tiles = upper_rows.shape[0]
    device_count = SLOTS // SLOT_DEV
    chosen = jax.random.permutation(key_order, total_tiles)[:SLOTS]
    first_block = jnp.asarray(upper_rows, jnp.int32)[chosen]
    second_block = jnp.asarray(upper_cols, jnp.int32)[chosen]
    live_counts = jax.random.randint(key_live, (device_count,), 2, SLOT_DEV + 1)
    fullest = jax.random.randint(key_full, (), 0, device_count)
    live_counts = jnp.where(jnp.arange(device_count) == fullest, SLOT_DEV, live_counts)
    used = (jnp.arange(SLOT_DEV)[None, :] < live_counts[:, None]).reshape(-1)
    first_block = jnp.where(used, first_block, -1)
    second_block = jnp.where(used, second_block, -1)
    return jnp.stack([first_block, second_block], 1).astype(jnp.int32)


def block_levels(key, shape, cuts, least, high):
    level = 1.0
    for dim, blocks in cuts:
        steps = jax.random.uniform(jax.random.fold_in(jax.random.fold_in(key, 6), dim), (blocks,), jnp.float32, least / len(cuts), high / len(cuts))
        level = level * jnp.repeat(jnp.exp(steps), shape[dim] // blocks).reshape((-1,) + (1,) * (len(shape) - 1 - dim))
    return level


def scatter_about(stream_key, shape, deviation, most, cuts=(), held_as=jnp.bfloat16):
    gain = block_levels(stream_key, shape, cuts, -0.22, 0.18) if cuts else 1.0
    values = jax.random.normal(stream_key, shape, jnp.float32) * deviation * gain
    return jnp.minimum(jnp.maximum(values, -most), most).astype(held_as)


def setup_inputs(seed: int = 0) -> dict:
    key_of = jax.random.split(jax.random.key(seed), 4)
    return {
        "states": draw_states(jax.random.fold_in(key_of[3], 71), 0),
        "derivatives": scatter_about(key_of[1], (SNAPS, R), 1.0, 6.0, ((0, 256),), jnp.float32),
        "tile_map": draw_tile_map(jax.random.fold_in(key_of[3], 71), 0),
    }


precise_mode = lax.Precision.HIGHEST


def doubled_states(states):
    unit_column = jnp.ones((states.shape[0], 1), states.dtype)
    extended = jnp.concatenate([states, unit_column], 1)
    return jnp.concatenate([extended, extended], 1)


def feature_tile(doubled, tile_index, tile_width):
    block_width = doubled.shape[1] // 2
    feature_count = block_width * ((block_width + 1) // 2)
    columns = tile_index.astype(jnp.int32) * tile_width + jnp.arange(tile_width, dtype=jnp.int32)
    valid = columns < feature_count
    safe_columns = jnp.where(valid, columns, 0).astype(jnp.int32)
    shift_part = (safe_columns // block_width).astype(jnp.int32)
    state_part = (safe_columns % block_width).astype(jnp.int32)
    left_values = jnp.take(doubled, state_part, axis=1)
    right_values = jnp.take(doubled, (state_part + shift_part).astype(jnp.int32), axis=1)
    return jnp.where(valid[None, :], left_values * right_values, jnp.zeros_like(left_values))


def inner_product(left_block, right_block):
    return lax.dot_general(left_block, right_block, (((0,), (0,)), ((), ())), precision=precise_mode, preferred_element_type=jnp.float32)


def reference(states, derivatives, tile_map):
    doubled = doubled_states(states)
    inv_snaps = 1.0 / SNAPS

    def one_tile(slot_pair):
        first_tile = jnp.maximum(slot_pair[0], 0)
        second_tile = jnp.maximum(slot_pair[1], 0)
        gram_tile = inner_product(feature_tile(doubled, first_tile, TW), feature_tile(doubled, second_tile, TW)) * inv_snaps
        return jnp.where(slot_pair[0] >= 0, gram_tile, jnp.zeros_like(gram_tile))

    gram_tiles = lax.map(one_tile, tile_map)

    def one_rhs(tile_index):
        return inner_product(feature_tile(doubled, tile_index, TW), derivatives) * inv_snaps

    rhs_tiles = jnp.arange(N_ROW * N_COL, dtype=jnp.int32) % CTILES
    rhs_blocks = lax.map(one_rhs, rhs_tiles)
    return gram_tiles, rhs_blocks
```

```python
import functools

import jax
import jax.numpy as jnp
from jax import lax
from jax.experimental import pallas as pl
from jax.experimental.pallas import tpu as pltpu
from jax.sharding import PartitionSpec as P

TW = 256
CTILES = 114
LANES = 128
MESH = pl.DeviceIdType.MESH
NT = (((1,), (1,)), ((), ()))
NN = (((1,), (0,)), ((), ()))
HIGH = lax.Precision.HIGH


def ring_slots(nz):
    up = {d: 2 * d - 1 for d in range(1, nz // 2 + 1)}
    down = {d: 2 * d for d in range(1, (nz + 1) // 2)}
    return up, down


def tile_place(tile, width):
    column = tile * TW
    shift = lax.div(column, width)
    first = column - shift * width
    second = first + shift
    second = jnp.where(second >= width, second - width, second)
    return column, first, second


def tile_masks(column, first, width, features):
    rows = lax.broadcasted_iota(jnp.int32, (TW, LANES), 0)
    return rows >= width - first, rows >= 2 * width - first, rows + column < features


def feature_part(feat, plane, first, second, masks):
    wrap_one, wrap_two, valid = masks
    left = feat[plane, pl.ds(first, TW), :]
    right = jnp.where(wrap_one, feat[plane, pl.ds(second + 1, TW), :], feat[plane, pl.ds(second, TW), :])
    last = jnp.where(wrap_two[TW - 16 :], feat[plane, pl.ds(second + 2 + TW - 16, 16), :], right[TW - 16 :])
    product = left * jnp.concatenate([right[: TW - 16], last], 0)
    tail = jnp.where(valid[TW - 32 :], product[TW - 32 :], 0.0)
    return jnp.concatenate([product[: TW - 32], tail], 0)


def kernel(sizes, map_ref, states_ref, derivs_ref, gram_ref, rhs_ref, own, halves, land, column, derivs, feat, sems):
    nzh, nzl, ncol, block, states, features = sizes
    nz = nzh * nzl
    width = states + 1
    half = states // nzh
    per_slot = 2 * ncol * block // LANES
    up_slot, down_slot = ring_slots(nz)
    zh, row, col = lax.axis_index("snap"), lax.axis_index("row"), lax.axis_index("col")
    core = lax.rem(row, 2)
    z = zh * nzl + lax.div(row, 2)
    inv_snaps = 1.0 / (nz * 2 * ncol * block)

    def device(z_to, core_to, col_to):
        return {"snap": lax.div(z_to, nzl), "row": lax.rem(z_to, nzl) * 2 + core_to, "col": col_to}

    def along_z(e):
        return device(lax.rem(z + e + nz, nz), core, col)

    def in_plane(k):
        return device(z, core, lax.rem(col + k, ncol))

    sibling = device(z, 1 - core, col)

    def copy(src, dst, kind, index, to):
        send, recv = sems[kind]
        return pltpu.make_async_remote_copy(
            src_ref=src, dst_ref=dst, send_sem=send.at[index], recv_sem=recv.at[index], device_id=to, device_id_type=MESH
        )

    barrier = pltpu.get_barrier_semaphore()

    def greet(to):
        pl.semaphore_signal(barrier, inc=1, device_id=to, device_id_type=MESH)

    greet(sibling)
    lax.fori_loop(1, nz, lambda e, c: (greet(along_z(e)), c)[1], 0)
    lax.fori_loop(1, ncol, lambda k, c: (greet(in_plane(k)), c)[1], 0)

    own[...] = jnp.ones(own.shape, jnp.float32)
    own[:, :states] = states_ref[...]
    for h in range(nzh):
        halves[h] = jnp.zeros((block, LANES), jnp.float32)
        halves[h, :, :half] = derivs_ref[:, h * half : (h + 1) * half]
    land[0, 0, col] = own[...]
    column[0] = halves[zh]

    pl.semaphore_wait(barrier, 1 + (nz - 1) + (ncol - 1))

    def plane_copy(k):
        return copy(own, land.at[0, 0, col], "plane", k, in_plane(k))

    lax.fori_loop(1, ncol, lambda k, c: (plane_copy(k).start(), c)[1], 0)

    def column_copy(e):
        slot = up_slot[e] if e in up_slot else down_slot[nz - e]
        z_to = lax.rem(z + e, nz)
        return copy(halves.at[lax.div(z_to, nzl)], column.at[slot], "column", slot, along_z(e))

    for e in range(1, nz):
        column_copy(e).start()

    def up_copy(d):
        return copy(land.at[up_slot[d - 1] if d > 1 else 0, 0], land.at[up_slot[d], 0], "ring", up_slot[d], along_z(1))

    def down_copy(d):
        return copy(land.at[down_slot[d - 1] if d > 1 else 0, 0], land.at[down_slot[d], 0], "ring", down_slot[d], along_z(-1))

    def sibling_copy(slot):
        return copy(land.at[slot, 0], land.at[slot, 1], "sibling", slot, sibling)

    def spread_copy(k):
        return copy(column, derivs.at[0, :, col], "spread", k, in_plane(k))

    def across_copy():
        return copy(derivs.at[0], derivs.at[1], "across", 0, sibling)

    def ring_copies(d):
        return [c(d) for c, slots in ((up_copy, up_slot), (down_copy, down_slot)) if d in slots]

    def slots_at(d):
        return [s[d] for s in (up_slot, down_slot) if d in s]

    def transpose(slots):
        def one(n, carry):
            slot, part = slots[0] + lax.div(n, per_slot), lax.rem(n, per_slot)
            plane = slots[0] * per_slot + n
            per_core = per_slot // 2
            blocks = LANES // block
            which = pl.ds(lax.rem(part, per_core) * blocks, blocks)
            tile = land[slot, lax.div(part, per_core), which].reshape(LANES, 2 * LANES)
            turned = jnp.concatenate([tile[:, :LANES].T, tile[:, LANES:].T], 0)[:width]
            feat[plane, :width] = turned
            feat[plane, width : 2 * width] = turned
            feat[plane, 2 * width : 2 * width + 24] = turned[:24]
            return carry

        lax.fori_loop(0, len(slots) * per_slot, one, 0)

    def tile_value(tile, planes):
        at, first, second = tile_place(tile, width)
        masks = tile_masks(at, first, width, features)
        return jnp.concatenate([feature_part(feat, plane, first, second, masks) for plane in planes], 1)

    def gram(slots, first_time, last_time):
        planes = [s * per_slot + i for s in slots for i in range(per_slot)]

        def one(p, carry):
            a, b = map_ref[p, 0], map_ref[p, 1]
            term = lax.dot_general(
                tile_value(jnp.maximum(a, 0), planes),
                tile_value(jnp.maximum(b, 0), planes),
                NT,
                precision=HIGH,
                preferred_element_type=jnp.float32,
            )
            total = term if first_time else gram_ref[p] + term
            if last_time:
                total = jnp.where(a >= 0, total * inv_snaps, 0.0)
            gram_ref[p] = total
            return carry

        lax.fori_loop(0, gram_ref.shape[0], one, 0)

    far = nz // 2
    lax.fori_loop(1, ncol, lambda k, c: (plane_copy(k).wait_recv(), c)[1], 0)
    for c in ring_copies(1):
        c.start()
    sibling_copy(0).start()
    for slot in range(1, nz):
        copy(halves.at[0], column.at[slot], "column", slot, sibling).wait_recv()
    derivs[0, :, col] = column[...]
    lax.fori_loop(1, ncol, lambda k, c: (spread_copy(k).start(), c)[1], 0)
    sibling_copy(0).wait_recv()
    transpose([0])
    gram([0], True, False)
    ready = []
    for d in range(1, far + 1):
        for c in ring_copies(d):
            c.wait_recv()
        for slot in slots_at(d):
            sibling_copy(slot).start()
        if d < far:
            for c in ring_copies(d + 1):
                c.start()
        if d == far - 1:
            lax.fori_loop(1, ncol, lambda k, c: (spread_copy(k).wait_recv(), c)[1], 0)
            across_copy().start()
        for slot in slots_at(d):
            sibling_copy(slot).wait_recv()
        transpose(slots_at(d))
        gram(slots_at(d), False, d == far)

    across_copy().wait_recv()
    rhs_tile = lax.rem(row * ncol + col, CTILES)
    planes = range(nz * per_slot)
    halves_of = [derivs[c, s].reshape(ncol * block, LANES) for s in range(nz) for c in range(2)]
    total = lax.dot_general(
        tile_value(rhs_tile, planes), jnp.concatenate(halves_of, 0), NN, precision=HIGH, preferred_element_type=jnp.float32
    )
    rhs_ref[0] = total[:, :half] * inv_snaps

    lax.fori_loop(1, ncol, lambda k, c: (plane_copy(k).wait_send(), c)[1], 0)
    lax.fori_loop(1, ncol, lambda k, c: (spread_copy(k).wait_send(), c)[1], 0)
    for e in range(1, nz):
        column_copy(e).wait_send()
    for d in range(1, far + 1):
        for c in ring_copies(d):
            c.wait_send()
    for slot in range(nz):
        sibling_copy(slot).wait_send()
    across_copy().wait_send()


KINDS = ("plane", "column", "ring", "sibling", "spread", "across")


def entry(sizes, *refs):
    refs, flat = refs[: -2 * len(KINDS)], refs[-2 * len(KINDS) :]
    kernel(sizes, *refs, {k: flat[2 * i : 2 * i + 2] for i, k in enumerate(KINDS)})


def local(nzh, nzl, ncol, states, derivatives, tile_map):
    block, width = states.shape
    nz = nzh * nzl
    planes = nz * 2 * ncol * block // LANES
    features = (width + 1) * ((width + 2) // 2)
    slots = tile_map.shape[0]
    counts = {"plane": ncol, "column": nz, "ring": nz, "sibling": nz, "spread": ncol, "across": 1}
    return pl.pallas_call(
        functools.partial(entry, (nzh, nzl, ncol, block, width, features)),
        out_shape=(
            jax.ShapeDtypeStruct((slots, TW, TW), jnp.float32),
            jax.ShapeDtypeStruct((1, TW, width // nzh), jnp.float32),
        ),
        in_specs=[
            pl.BlockSpec(memory_space=pltpu.SMEM),
            pl.BlockSpec(memory_space=pltpu.VMEM),
            pl.BlockSpec(memory_space=pltpu.VMEM),
        ],
        out_specs=[pl.BlockSpec(memory_space=pltpu.VMEM)] * 2,
        scratch_shapes=[
            pltpu.VMEM((block, 2 * LANES), jnp.float32),
            pltpu.VMEM((nzh, block, LANES), jnp.float32),
            pltpu.VMEM((nz, 2, ncol, block, 2 * LANES), jnp.float32),
            pltpu.VMEM((nz, block, LANES), jnp.float32),
            pltpu.VMEM((2, nz, ncol, block, LANES), jnp.float32),
            pltpu.VMEM((planes, 2 * (width + 1) + 24, LANES), jnp.float32),
        ]
        + [pltpu.SemaphoreType.DMA((counts[k],)) for k in KINDS for _ in range(2)],
        compiler_params=pltpu.CompilerParams(collective_id=0, has_side_effects=True, vmem_limit_bytes=56 * 2**20),
    )(tile_map, states, derivatives)


def solution(mesh):
    nzh, rows, ncol = mesh.shape["snap"], mesh.shape["row"], mesh.shape["col"]
    placed = P(("snap", "row", "col"), None)
    return jax.shard_map(
        functools.partial(local, nzh, rows // 2, ncol),
        mesh=mesh,
        in_specs=(placed, placed, placed),
        out_specs=(P(("snap", "row", "col"), None, None), P(("row", "col"), None, "snap")),
        check_vma=False,
    )
```

```python
import functools

import jax
import jax.numpy as jnp
from jax import lax
from jax.experimental import pallas as pl
from jax.experimental.pallas import tpu as pltpu
from jax.sharding import PartitionSpec as P

TW = 256
CTILES = 114
LANES = 128
GROUP = 16
LEAD = GROUP - 1
COPIES = 536
MESH = pl.DeviceIdType.MESH
NT = (((1,), (1,)), ((), ()))
NN = (((1,), (0,)), ((), ()))
HIGH = lax.Precision.HIGH


def ring_slots(nz):
    up = {d: 2 * d - 1 for d in range(1, nz // 2 + 1)}
    down = {d: 2 * d for d in range(1, (nz + 1) // 2)}
    return up, down


def tile_place(tile, width):
    column = tile * TW
    shift = lax.div(column, width)
    first = column - shift * width
    second = first + shift
    second = jnp.where(second >= width, second - width, second)
    turn = lax.rem(first + GROUP - 1, GROUP)
    wrap = lax.div(width - first + turn, GROUP)
    return turn, wrap, first - turn + LEAD, second - turn + LEAD


def feature_part(feat, plane, place):
    turn, wrap, left, right = place
    rows = lax.broadcasted_iota(jnp.int32, (GROUP, LANES), 0)

    def read(start, size):
        return feat[plane, pl.ds(start, size), :]

    head_left = jnp.where(rows >= turn, read(left, GROUP), read(left + TW, GROUP))
    tail_right = jnp.where(rows >= GROUP * wrap - GROUP + 1, read(right + TW + 2, GROUP), read(right + TW + 1, GROUP))
    head_right = jnp.where(rows >= turn, read(right, GROUP), tail_right)
    body_left = read(left + GROUP, TW - GROUP)
    body_right = [read(right + GROUP * g + jnp.where(g >= wrap, 1, 0), GROUP) for g in range(1, TW // GROUP)]
    return jnp.concatenate([head_left * head_right, body_left * jnp.concatenate(body_right, 0)], 0)


def turn_rows(turned, value, turn):
    for h in range(value.shape[1] // LANES):
        part = value[:, h * LANES : (h + 1) * LANES]
        turned[h, :TW] = part
        turned[h, TW:] = part[:GROUP]
    return jnp.concatenate([turned[h, pl.ds(turn, TW), :] for h in range(value.shape[1] // LANES)], 1)


def pair_places(map_ref, p, width):
    return [tile_place(jnp.maximum(map_ref[q, p], 0), width) for q in range(2)]


def finish(width, features, inv_snaps, map_ref, turned_ref, rhs_in_ref, gram_ref, rhs_ref, turned):
    p = pl.program_id(0)
    (a, *_), (b, *_) = pair_places(map_ref, p, width)
    total = pltpu.roll(turn_rows(turned, turned_ref[0], a), lax.rem(TW - b, TW), 1)
    row_at = lax.broadcasted_iota(jnp.int32, (TW, TW), 0) + map_ref[0, p] * TW
    col_at = lax.broadcasted_iota(jnp.int32, (TW, TW), 1) + map_ref[1, p] * TW
    live = (map_ref[0, p] >= 0) & (row_at < features) & (col_at < features)
    gram_ref[0] = jnp.where(live, total * inv_snaps, 0.0)

    @pl.when(p == 0)
    def _():
        rhs_ref[...] = rhs_in_ref[...]


def kernel(sizes, map_ref, states_ref, derivs_ref, gram_ref, rhs_ref, own, halves, plane_rows, land, column, derivs, feat, turned, sems):
    nzh, nzl, ncol, block, states, features = sizes
    nz = nzh * nzl
    width = states + 1
    half = states // nzh
    per_core = ncol * block // LANES
    per_slot = 2 * per_core
    up_slot, down_slot = ring_slots(nz)
    zh, row, col = lax.axis_index("snap"), lax.axis_index("row"), lax.axis_index("col")
    core = lax.rem(row, 2)
    z = zh * nzl + lax.div(row, 2)
    inv_snaps = 1.0 / (nz * 2 * ncol * block)

    def device(z_to, core_to, col_to):
        return {"snap": lax.div(z_to, nzl), "row": lax.rem(z_to, nzl) * 2 + core_to, "col": col_to}

    def along_z(e):
        return device(lax.rem(z + e + nz, nz), core, col)

    def in_plane(k):
        return device(z, core, lax.rem(col + k, ncol))

    sibling = device(z, 1 - core, col)

    def copy(src, dst, kind, index, to):
        send, recv = sems[kind]
        return pltpu.make_async_remote_copy(
            src_ref=src, dst_ref=dst, send_sem=send.at[index], recv_sem=recv.at[index], device_id=to, device_id_type=MESH
        )

    barrier = pltpu.get_barrier_semaphore()

    def greet(to):
        pl.semaphore_signal(barrier, inc=1, device_id=to, device_id_type=MESH)

    greet(sibling)
    lax.fori_loop(1, nz, lambda e, c: (greet(along_z(e)), c)[1], 0)
    lax.fori_loop(1, ncol, lambda k, c: (greet(in_plane(k)), c)[1], 0)

    own[...] = jnp.ones(own.shape, jnp.float32)
    own[:, :states] = states_ref[...]
    for h in range(nzh):
        halves[h] = jnp.zeros((block, LANES), jnp.float32)
        halves[h, :, :half] = derivs_ref[:, h * half : (h + 1) * half]
    plane_rows[col] = own[...]
    column[0] = halves[zh]

    pl.semaphore_wait(barrier, 1 + (nz - 1) + (ncol - 1))

    def plane_copy(k):
        return copy(own, plane_rows.at[col], "plane", k, in_plane(k))

    lax.fori_loop(1, ncol, lambda k, c: (plane_copy(k).start(), c)[1], 0)

    def column_copy(e):
        slot = up_slot[e] if e in up_slot else down_slot[nz - e]
        z_to = lax.rem(z + e, nz)
        return copy(halves.at[lax.div(z_to, nzl)], column.at[slot], "column", slot, along_z(e))

    for e in range(1, nz):
        column_copy(e).start()

    def up_copy(d):
        return copy(land.at[up_slot[d - 1] if d > 1 else 0, 0], land.at[up_slot[d], 0], "ring", up_slot[d], along_z(1))

    def down_copy(d):
        return copy(land.at[down_slot[d - 1] if d > 1 else 0, 0], land.at[down_slot[d], 0], "ring", down_slot[d], along_z(-1))

    def sibling_copy(slot):
        return copy(land.at[slot, 0], land.at[slot, 1], "sibling", slot, sibling)

    def spread_copy(k):
        return copy(column, derivs.at[0, :, col], "spread", k, in_plane(k))

    def across_copy():
        return copy(derivs.at[0], derivs.at[1], "across", 0, sibling)

    def ring_copies(d):
        return [c(d) for c, slots in ((up_copy, up_slot), (down_copy, down_slot)) if d in slots]

    def slots_at(d):
        return [s[d] for s in (up_slot, down_slot) if d in s]

    def turn_plane():
        blocks = LANES // block
        for n in range(per_core):
            tile = plane_rows[n * blocks : (n + 1) * blocks].reshape(LANES, 2 * LANES)
            land[0, 0, n] = jnp.concatenate([tile[:, :LANES].T, tile[:, LANES:].T], 0)

    def unfold(slots):
        def one(n, carry):
            slot, part = slots[0] + lax.div(n, per_slot), lax.rem(n, per_slot)
            rows = land[slot, lax.div(part, per_core), lax.rem(part, per_core)][:width]
            plane = slots[0] * per_slot + n
            feat[plane, :LEAD] = rows[width - LEAD :]
            feat[plane, LEAD : LEAD + width] = rows
            feat[plane, LEAD + width : LEAD + 2 * width] = rows
            feat[plane, LEAD + 2 * width :] = rows[: COPIES - LEAD - 2 * width]
            return carry

        lax.fori_loop(0, len(slots) * per_slot, one, 0)

    def tile_value(place, planes):
        return jnp.concatenate([feature_part(feat, plane, place) for plane in planes], 1)

    def gram(slots, first_time):
        planes = [s * per_slot + i for s in slots for i in range(per_slot)]

        def one(p, carry):
            a, b = pair_places(map_ref, p, width)
            term = lax.dot_general(
                tile_value(a, planes), tile_value(b, planes), NT, precision=HIGH, preferred_element_type=jnp.float32
            )
            gram_ref[p] = term if first_time else gram_ref[p] + term
            return carry

        lax.fori_loop(0, gram_ref.shape[0], one, 0, unroll=2)

    far = nz // 2
    lax.fori_loop(1, ncol, lambda k, c: (plane_copy(k).wait_recv(), c)[1], 0)
    turn_plane()
    for c in ring_copies(1):
        c.start()
    sibling_copy(0).start()
    for slot in range(1, nz):
        copy(halves.at[0], column.at[slot], "column", slot, sibling).wait_recv()
    derivs[0, :, col] = column[...]
    lax.fori_loop(1, ncol, lambda k, c: (spread_copy(k).start(), c)[1], 0)
    sibling_copy(0).wait_recv()
    unfold([0])
    gram([0], True)
    ready = []
    for d in range(1, far + 1):
        for c in ring_copies(d):
            c.wait_recv()
        for slot in slots_at(d):
            sibling_copy(slot).start()
        if d < far:
            for c in ring_copies(d + 1):
                c.start()
        if d == far - 1:
            lax.fori_loop(1, ncol, lambda k, c: (spread_copy(k).wait_recv(), c)[1], 0)
            across_copy().start()
        for slot in slots_at(d):
            sibling_copy(slot).wait_recv()
        unfold(slots_at(d))
        gram(slots_at(d), False)

    across_copy().wait_recv()
    rhs_tile = lax.rem(row * ncol + col, CTILES)
    place = tile_place(rhs_tile, width)
    planes = range(nz * per_slot)
    parts = [derivs[c, s].reshape(ncol * block, LANES) for s in range(nz) for c in range(2)]
    total = lax.dot_general(
        tile_value(place, planes), jnp.concatenate(parts, 0), NN, precision=HIGH, preferred_element_type=jnp.float32
    )
    total = turn_rows(turned, total, place[0])
    row_at = lax.broadcasted_iota(jnp.int32, total.shape, 0) + rhs_tile * TW
    total = jnp.where(row_at < features, total * inv_snaps, 0.0)
    turned_rhs = jnp.concatenate([total[:LANES].T, total[LANES:].T], 1)
    rhs_ref[0] = turned_rhs[:half]

    lax.fori_loop(1, ncol, lambda k, c: (plane_copy(k).wait_send(), c)[1], 0)
    lax.fori_loop(1, ncol, lambda k, c: (spread_copy(k).wait_send(), c)[1], 0)
    for e in range(1, nz):
        column_copy(e).wait_send()
    for d in range(1, far + 1):
        for c in ring_copies(d):
            c.wait_send()
    for slot in range(nz):
        sibling_copy(slot).wait_send()
    across_copy().wait_send()


KINDS = ("plane", "column", "ring", "sibling", "spread", "across")


def entry(sizes, *refs):
    refs, flat = refs[: -2 * len(KINDS)], refs[-2 * len(KINDS) :]
    kernel(sizes, *refs, {k: flat[2 * i : 2 * i + 2] for i, k in enumerate(KINDS)})


def local(nzh, nzl, ncol, states, derivatives, tile_map):
    block, width = states.shape
    nz = nzh * nzl
    planes = nz * 2 * ncol * block // LANES
    features = (width + 1) * ((width + 2) // 2)
    slots = tile_map.shape[0]
    counts = {"plane": ncol, "column": nz, "ring": nz, "sibling": nz, "spread": ncol, "across": 1}
    gram_tiles, rhs = pl.pallas_call(
        functools.partial(entry, (nzh, nzl, ncol, block, width, features)),
        out_shape=(
            jax.ShapeDtypeStruct((slots, TW, TW), jnp.float32),
            jax.ShapeDtypeStruct((1, width // nzh, TW), jnp.float32),
        ),
        in_specs=[
            pl.BlockSpec(memory_space=pltpu.SMEM),
            pl.BlockSpec(memory_space=pltpu.VMEM),
            pl.BlockSpec(memory_space=pltpu.VMEM),
        ],
        out_specs=[pl.BlockSpec(memory_space=pltpu.VMEM)] * 2,
        scratch_shapes=[
            pltpu.VMEM((block, 2 * LANES), jnp.float32),
            pltpu.VMEM((nzh, block, LANES), jnp.float32),
            pltpu.VMEM((ncol, block, 2 * LANES), jnp.float32),
            pltpu.VMEM((nz, 2, ncol * block // LANES, 2 * LANES, LANES), jnp.float32),
            pltpu.VMEM((nz, block, LANES), jnp.float32),
            pltpu.VMEM((2, nz, ncol, block, LANES), jnp.float32),
            pltpu.VMEM((planes, COPIES, LANES), jnp.float32),
            pltpu.VMEM((2, TW + GROUP, LANES), jnp.float32),
        ]
        + [pltpu.SemaphoreType.DMA((counts[k],)) for k in KINDS for _ in range(2)],
        compiler_params=pltpu.CompilerParams(collective_id=0, has_side_effects=True, vmem_limit_bytes=40 * 2**20),
    )(tile_map.T, states, derivatives)
    tile = pl.BlockSpec((1, TW, TW), lambda p: (p, 0, 0))
    side = pl.BlockSpec((1, width // nzh, TW), lambda p: (0, 0, 0))
    gram_tiles, rhs = pl.pallas_call(
        functools.partial(finish, width + 1, features, 1.0 / (nz * 2 * ncol * block)),
        grid=(slots,),
        out_shape=(
            jax.ShapeDtypeStruct((slots, TW, TW), jnp.float32),
            jax.ShapeDtypeStruct((1, width // nzh, TW), jnp.float32),
        ),
        in_specs=[pl.BlockSpec(memory_space=pltpu.SMEM), tile, side],
        out_specs=[tile, side],
        scratch_shapes=[pltpu.VMEM((2, TW + GROUP, LANES), jnp.float32)],
    )(tile_map.T, gram_tiles, rhs)
    return gram_tiles, rhs.transpose(0, 2, 1)


def solution(mesh):
    nzh, rows, ncol = mesh.shape["snap"], mesh.shape["row"], mesh.shape["col"]
    placed = P(("snap", "row", "col"), None)
    return jax.shard_map(
        functools.partial(local, nzh, rows // 2, ncol),
        mesh=mesh,
        in_specs=(placed, placed, placed),
        out_specs=(P(("snap", "row", "col"), None, None), P(("row", "col"), None, "snap")),
        check_vma=False,
    )
```

```python
import functools

import jax
import jax.numpy as jnp
from jax import lax
from jax.experimental import pallas as pl
from jax.experimental.pallas import tpu as pltpu
from jax.sharding import PartitionSpec as P

TW = 256
CTILES = 114
LANES = 128
GROUP = 16
LEAD = GROUP - 1
COPIES = 536
MESH = pl.DeviceIdType.MESH
NT = (((1,), (1,)), ((), ()))
NN = (((1,), (0,)), ((), ()))
HIGH = lax.Precision.HIGH


def ring_slots(nz):
    up = {d: 2 * d - 1 for d in range(1, nz // 2 + 1)}
    down = {d: 2 * d for d in range(1, (nz + 1) // 2)}
    return up, down


def tile_place(tile, width):
    column = tile * TW
    shift = lax.div(column, width)
    first = column - shift * width
    second = first + shift
    second = jnp.where(second >= width, second - width, second)
    turn = lax.rem(first + GROUP - 1, GROUP)
    wrap = lax.div(width - first + turn, GROUP)
    return turn, wrap, first - turn + LEAD, second - turn + LEAD


def feature_part(feat, plane, place):
    turn, wrap, left, right = place
    rows = lax.broadcasted_iota(jnp.int32, (GROUP, LANES), 0)

    def read(start, size):
        return feat[plane, pl.ds(start, size), :]

    head_left = jnp.where(rows >= turn, read(left, GROUP), read(left + TW, GROUP))
    tail_right = jnp.where(rows >= GROUP * wrap - GROUP + 1, read(right + TW + 2, GROUP), read(right + TW + 1, GROUP))
    head_right = jnp.where(rows >= turn, read(right, GROUP), tail_right)
    body_left = read(left + GROUP, TW - GROUP)
    body_right = [read(right + GROUP * g + jnp.where(g >= wrap, 1, 0), GROUP) for g in range(1, TW // GROUP)]
    return jnp.concatenate([head_left * head_right, body_left * jnp.concatenate(body_right, 0)], 0)


def turn_rows(turned, value, turn):
    for h in range(value.shape[1] // LANES):
        part = value[:, h * LANES : (h + 1) * LANES]
        turned[h, :TW] = part
        turned[h, TW:] = part[:GROUP]
    return jnp.concatenate([turned[h, pl.ds(turn, TW), :] for h in range(value.shape[1] // LANES)], 1)


def pair_places(map_ref, p, width):
    return [tile_place(jnp.maximum(map_ref[q, p], 0), width) for q in range(2)]


def finish(width, features, inv_snaps, map_ref, turned_ref, rhs_in_ref, gram_ref, rhs_ref, taken, given, turned, side, took, gave, rhs_sem):
    slots = taken.shape[0]
    rhs_take = pltpu.make_async_copy(rhs_in_ref, side, rhs_sem.at[0])
    rhs_give = pltpu.make_async_copy(side, rhs_ref, rhs_sem.at[1])
    rhs_take.start()

    def take(p):
        return pltpu.make_async_copy(turned_ref.at[p], taken.at[p], took.at[p])

    def give(p):
        return pltpu.make_async_copy(given.at[p], gram_ref.at[p], gave.at[p])

    for p in range(slots):
        take(p).start()

    def one(p, carry):
        take(p).wait()
        (a, *_), (b, *_) = pair_places(map_ref, p, width)
        total = pltpu.roll(turn_rows(turned, taken[p], a), lax.rem(TW - b, TW), 1)
        row_at = lax.broadcasted_iota(jnp.int32, (TW, TW), 0) + map_ref[0, p] * TW
        col_at = lax.broadcasted_iota(jnp.int32, (TW, TW), 1) + map_ref[1, p] * TW
        live = (map_ref[0, p] >= 0) & (row_at < features) & (col_at < features)
        given[p] = jnp.where(live, total * inv_snaps, 0.0)
        give(p).start()
        return carry

    lax.fori_loop(0, slots, one, 0)
    rhs_take.wait()
    rhs_give.start()
    rhs_give.wait()
    for p in range(slots):
        give(p).wait()


def turn_plane(tile):
    return jnp.concatenate([tile[:, :LANES].T, tile[:, LANES:].T], 0)


def kernel(sizes, map_ref, states_ref, derivs_ref, gram_ref, rhs_ref, bufs, sems):
    nzh, nzl, ncol, block, states, features = sizes
    nz = nzh * nzl
    far = nz // 2
    width = states + 1
    half = states // nzh
    slots = gram_ref.shape[0]
    per_core = ncol * block // LANES
    up_slot, down_slot = ring_slots(nz)
    zh, row, col = lax.axis_index("snap"), lax.axis_index("row"), lax.axis_index("col")
    core = lax.rem(row, 2)
    z = zh * nzl + lax.div(row, 2)
    inv_snaps = 1.0 / (nz * 2 * ncol * block)
    own, halves, plane_rows, column = bufs["own"], bufs["halves"], bufs["plane_rows"], bufs["column"]
    land, derivs, feat, turned = bufs["land"], bufs["derivs"], bufs["feat"], bufs["turned"]

    def device(z_to, core_to, col_to):
        return {"snap": lax.div(z_to, nzl), "row": lax.rem(z_to, nzl) * 2 + core_to, "col": col_to}

    def along_z(e):
        return device(lax.rem(z + e + nz, nz), core, col)

    def in_plane(k):
        return device(z, core, lax.rem(col + k, ncol))

    sibling = device(z, 1 - core, col)

    def copy(src, dst, kind, index, to):
        send, recv = sems[kind]
        return pltpu.make_async_remote_copy(
            src_ref=src, dst_ref=dst, send_sem=send.at[index], recv_sem=recv.at[index], device_id=to, device_id_type=MESH
        )

    def each(first, last, act):
        lax.fori_loop(first, last, lambda k, c: (act(k), c)[1], 0)

    load_states = pltpu.make_async_copy(states_ref, bufs["states"], sems["load"][0].at[0])
    load_derivs = pltpu.make_async_copy(derivs_ref, bufs["given"], sems["load"][1].at[0])
    load_states.start()
    load_derivs.start()
    barrier = pltpu.get_barrier_semaphore()

    def greet(to):
        pl.semaphore_signal(barrier, inc=1, device_id=to, device_id_type=MESH)

    greet(sibling)
    each(1, nz, lambda e: greet(along_z(e)))
    each(1, ncol, lambda k: greet(in_plane(k)))

    load_states.wait()
    load_derivs.wait()
    own[...] = jnp.ones(own.shape, jnp.float32)
    own[:, :states] = bufs["states"][...]
    for h in range(nzh):
        halves[h] = jnp.zeros((block, LANES), jnp.float32)
        halves[h, :, :half] = bufs["given"][:, h * half : (h + 1) * half]
    plane_rows[col] = own[...]
    column[0] = halves[zh]

    pl.semaphore_wait(barrier, 1 + (nz - 1) + (ncol - 1))

    def plane_copy(k):
        return copy(own, plane_rows.at[col], "plane", k, in_plane(k))

    def column_copy(e):
        slot = up_slot[e] if e in up_slot else down_slot[nz - e]
        z_to = lax.rem(z + e, nz)
        return copy(halves.at[lax.div(z_to, nzl)], column.at[slot], "column", slot, along_z(e))

    def spread_copy(k):
        return copy(column, derivs.at[0, :, col], "spread", k, in_plane(k))

    def across_copy():
        return copy(derivs.at[0], derivs.at[1], "across", 0, sibling)

    def ring_copies(d, n):
        copies = []
        for slot_of, way, takes in ((up_slot, 1, n < (per_core + 1) // 2), (down_slot, -1, n >= (per_core + 1) // 2)):
            if d < far or (d == far and takes):
                src = slot_of[d - 1] if d > 1 else 0
                dst = slot_of[d] if d < far else up_slot[far]
                copies.append(copy(land.at[src, 0, n], land.at[dst, 0, n], "ring", dst * per_core + n, along_z(way)))
        return copies

    def slots_at(d):
        return [0] if d == 0 else [s[d] for s in (up_slot, down_slot) if d in s]

    def share(slot, n):
        return copy(land.at[slot, 0, n], land.at[slot, 1, n], "share", slot * per_core + n, sibling)

    def pass_on(d, n):
        for c in ring_copies(d, n):
            c.wait_recv()
        for c in ring_copies(d + 1, n):
            c.start()
        for slot in slots_at(d):
            share(slot, n).start()

    def planes_of(d, ns):
        return [(s * 2 + c) * per_core + n for s in slots_at(d) for c in range(2) for n in ns]

    def unfold(d, ns):
        for slot in slots_at(d):
            for n in ns:
                share(slot, n).wait_recv()

        def one(m, carry):
            slot = slots_at(d)[0] + lax.div(m, 2 * len(ns))
            c, n = lax.rem(lax.div(m, len(ns)), 2), lax.rem(m, len(ns)) + ns[0]
            rows = land[slot, c, n][:width]
            plane = (slot * 2 + c) * per_core + n
            feat[plane, :LEAD] = rows[width - LEAD :]
            feat[plane, LEAD : LEAD + width] = rows
            feat[plane, LEAD + width : LEAD + 2 * width] = rows
            feat[plane, LEAD + 2 * width :] = rows[: COPIES - LEAD - 2 * width]
            return carry

        lax.fori_loop(0, len(slots_at(d)) * 2 * len(ns), one, 0)

    def tile_value(place, planes):
        return jnp.concatenate([feature_part(feat, plane, place) for plane in planes], 1)

    def gram(planes, first_time, midway=None):
        together = slots // 2

        def one(h, carry):
            if midway is not None:
                pl.when(h == 1)(midway)
            for j in range(together):
                p = h * together + j
                a, b = pair_places(map_ref, p, width)
                term = lax.dot_general(
                    tile_value(a, planes), tile_value(b, planes), NT, precision=HIGH, preferred_element_type=jnp.float32
                )
                gram_ref[p] = term if first_time else gram_ref[p] + term
            return carry

        lax.fori_loop(0, 2, one, 0)

    both = list(range(per_core))
    low, high = both[: (per_core + 1) // 2], both[(per_core + 1) // 2 :]

    def pass_all(d, ns):
        for n in ns:
            pass_on(d, n)

    each(1, ncol, lambda k: plane_copy(k).start())
    for e in range(1, nz):
        column_copy(e).start()
    each(1, ncol, lambda k: plane_copy(k).wait_recv())
    for n in both:
        land[0, 0, n] = turn_plane(plane_rows[...].reshape(per_core, LANES, 2 * LANES)[n])
        for c in ring_copies(1, n):
            c.start()
        share(0, n).start()
    for slot in range(1, nz):
        copy(halves.at[0], column.at[slot], "column", slot, sibling).wait_recv()
    derivs[0, :, col] = column[...]
    each(1, ncol, lambda k: spread_copy(k).start())

    unfold(0, both)
    gram(planes_of(0, both), True)
    pass_all(1, low)
    unfold(1, low)
    gram(planes_of(1, low), False, functools.partial(pass_all, 1, high))
    if high:
        unfold(1, high)
        gram(planes_of(1, high), False, functools.partial(pass_all, 2, low))
    else:
        pass_all(2, low)
    for d in range(2, far + 1):
        pass_all(d, high)
        if d == far:
            each(1, ncol, lambda k: spread_copy(k).wait_recv())
            across_copy().start()
        unfold(d, both)
        gram(planes_of(d, both), False, functools.partial(pass_all, d + 1, low) if d < far else None)

    across_copy().wait_recv()
    rhs_tile = lax.rem(row * ncol + col, CTILES)
    place = tile_place(rhs_tile, width)
    parts = [derivs[c, s].reshape(ncol * block, LANES) for s in range(nz) for c in range(2)]
    total = lax.dot_general(
        tile_value(place, range(nz * 2 * per_core)),
        jnp.concatenate(parts, 0),
        NN,
        precision=HIGH,
        preferred_element_type=jnp.float32,
    )
    total = turn_rows(turned, total, place[0])
    row_at = lax.broadcasted_iota(jnp.int32, total.shape, 0) + rhs_tile * TW
    total = jnp.where(row_at < features, total * inv_snaps, 0.0)
    turned_rhs = jnp.concatenate([total[:LANES].T, total[LANES:].T], 1)
    rhs_ref[0] = turned_rhs[:half]

    each(1, ncol, lambda k: plane_copy(k).wait_send())
    each(1, ncol, lambda k: spread_copy(k).wait_send())
    for e in range(1, nz):
        column_copy(e).wait_send()
    for n in both:
        for d in range(1, far + 1):
            for c in ring_copies(d, n):
                c.wait_send()
        for slot in range(nz):
            share(slot, n).wait_send()
    across_copy().wait_send()


def entry(sizes, names, kinds, *refs):
    refs, flat = refs[: -2 * len(kinds)], refs[-2 * len(kinds) :]
    refs, bufs = refs[: -len(names)], refs[-len(names) :]
    kernel(sizes, *refs, dict(zip(names, bufs)), {k: flat[2 * i : 2 * i + 2] for i, k in enumerate(kinds)})


def local(nzh, nzl, ncol, states, derivatives, tile_map):
    block, width = states.shape
    nz = nzh * nzl
    per_core = ncol * block // LANES
    features = (width + 1) * ((width + 2) // 2)
    slots = tile_map.shape[0]
    shapes = {
        "states": (block, width),
        "given": (block, width),
        "own": (block, 2 * LANES),
        "halves": (nzh, block, LANES),
        "plane_rows": (ncol, block, 2 * LANES),
        "column": (nz, block, LANES),
        "land": (nz, 2, per_core, 2 * LANES, LANES),
        "derivs": (2, nz, ncol, block, LANES),
        "feat": (nz * 2 * per_core, COPIES, LANES),
        "turned": (2, TW + GROUP, LANES),
    }
    counts = {
        "load": 1,
        "plane": ncol,
        "column": nz,
        "spread": ncol,
        "across": 1,
        "ring": nz * per_core,
        "share": nz * per_core,
    }
    out_shape = (
        jax.ShapeDtypeStruct((slots, TW, TW), jnp.float32),
        jax.ShapeDtypeStruct((1, width // nzh, TW), jnp.float32),
    )
    smem, vmem, anywhere = (pl.BlockSpec(memory_space=m) for m in (pltpu.SMEM, pltpu.VMEM, pl.ANY))
    gram_tiles, rhs = pl.pallas_call(
        functools.partial(entry, (nzh, nzl, ncol, block, width, features), tuple(shapes), tuple(counts)),
        out_shape=out_shape,
        in_specs=[smem, anywhere, anywhere],
        out_specs=[vmem, vmem],
        scratch_shapes=[pltpu.VMEM(shape, jnp.float32) for shape in shapes.values()]
        + [pltpu.SemaphoreType.DMA((count,)) for count in counts.values() for _ in range(2)],
        compiler_params=pltpu.CompilerParams(collective_id=0, has_side_effects=True, vmem_limit_bytes=60 * 2**20),
    )(tile_map.T, states, derivatives)
    gram_tiles, rhs = pl.pallas_call(
        functools.partial(finish, width + 1, features, 1.0 / (nz * 2 * ncol * block)),
        out_shape=out_shape,
        in_specs=[smem, anywhere, anywhere],
        out_specs=[anywhere, anywhere],
        scratch_shapes=[
            pltpu.VMEM((slots, TW, TW), jnp.float32),
            pltpu.VMEM((slots, TW, TW), jnp.float32),
            pltpu.VMEM((2, TW + GROUP, LANES), jnp.float32),
            pltpu.VMEM((1, width // nzh, TW), jnp.float32),
            pltpu.SemaphoreType.DMA((slots,)),
            pltpu.SemaphoreType.DMA((slots,)),
            pltpu.SemaphoreType.DMA((2,)),
        ],
        compiler_params=pltpu.CompilerParams(vmem_limit_bytes=60 * 2**20),
    )(tile_map.T, gram_tiles, rhs)
    return gram_tiles, rhs.transpose(0, 2, 1)


def solution(mesh):
    nzh, rows, ncol = mesh.shape["snap"], mesh.shape["row"], mesh.shape["col"]
    placed = P(("snap", "row", "col"), None)
    return jax.shard_map(
        functools.partial(local, nzh, rows // 2, ncol),
        mesh=mesh,
        in_specs=(placed, placed, placed),
        out_specs=(P(("snap", "row", "col"), None, None), P(("row", "col"), None, "snap")),
        check_vma=False,
    )
```

```python
import functools

import jax
import jax.numpy as jnp
from jax import lax
from jax.experimental import pallas as pl
from jax.experimental.pallas import tpu as pltpu
from jax.sharding import PartitionSpec as P

TW = 256
CTILES = 114
LANES = 128
GROUP = 16
LEAD = GROUP - 1
COPIES = 536
MESH = pl.DeviceIdType.MESH
NT = (((1,), (1,)), ((), ()))
NN = (((1,), (0,)), ((), ()))


def ring_slots(nz):
    up = {d: 2 * d - 1 for d in range(1, nz // 2 + 1)}
    down = {d: 2 * d for d in range(1, (nz + 1) // 2)}
    return up, down


def tile_place(tile, width):
    column = tile * TW
    shift = lax.div(column, width)
    first = column - shift * width
    second = first + shift
    second = jnp.where(second >= width, second - width, second)
    turn = lax.rem(first + GROUP - 1, GROUP)
    wrap = lax.div(width - first + turn, GROUP)
    return turn, wrap, first - turn + LEAD, second - turn + LEAD


def feature_part(feat, plane, place):
    turn, wrap, left, right = place
    rows = lax.broadcasted_iota(jnp.int32, (GROUP, LANES), 0)

    def read(start, size):
        return feat[plane, pl.ds(start, size), :]

    head_left = jnp.where(rows >= turn, read(left, GROUP), read(left + TW, GROUP))
    tail_right = jnp.where(rows >= GROUP * wrap - GROUP + 1, read(right + TW + 2, GROUP), read(right + TW + 1, GROUP))
    head_right = jnp.where(rows >= turn, read(right, GROUP), tail_right)
    body_left = read(left + GROUP, TW - GROUP)
    body_right = [read(right + GROUP * g + jnp.where(g >= wrap, 1, 0), GROUP) for g in range(1, TW // GROUP)]
    return jnp.concatenate([head_left * head_right, body_left * jnp.concatenate(body_right, 0)], 0)


def turn_rows(turned, value, turn):
    for h in range(value.shape[1] // LANES):
        part = value[:, h * LANES : (h + 1) * LANES]
        turned[h, :TW] = part
        turned[h, TW:] = part[:GROUP]
    return jnp.concatenate([turned[h, pl.ds(turn, TW), :] for h in range(value.shape[1] // LANES)], 1)


def pair_places(map_ref, p, width):
    return [tile_place(jnp.maximum(map_ref[q, p], 0), width) for q in range(2)]


def finish(width, features, inv_snaps, map_ref, turned_ref, rhs_in_ref, gram_ref, rhs_ref, taken, given, turned, side, took, gave, rhs_sem):
    slots = taken.shape[0]
    rhs_take = pltpu.make_async_copy(rhs_in_ref, side, rhs_sem.at[0])
    rhs_give = pltpu.make_async_copy(side, rhs_ref, rhs_sem.at[1])
    rhs_take.start()

    def take(p):
        return pltpu.make_async_copy(turned_ref.at[p], taken.at[p], took.at[p])

    def give(p):
        return pltpu.make_async_copy(given.at[p], gram_ref.at[p], gave.at[p])

    for p in range(slots):
        take(p).start()

    def one(p, carry):
        take(p).wait()
        (a, *_), (b, *_) = pair_places(map_ref, p, width)
        total = pltpu.roll(turn_rows(turned, taken[p], a), lax.rem(TW - b, TW), 1)
        row_at = lax.broadcasted_iota(jnp.int32, (TW, TW), 0) + map_ref[0, p] * TW
        col_at = lax.broadcasted_iota(jnp.int32, (TW, TW), 1) + map_ref[1, p] * TW
        live = (map_ref[0, p] >= 0) & (row_at < features) & (col_at < features)
        given[p] = jnp.where(live, total * inv_snaps, 0.0)
        give(p).start()
        return carry

    lax.fori_loop(0, slots, one, 0)
    rhs_take.wait()
    rhs_give.start()
    rhs_give.wait()
    for p in range(slots):
        give(p).wait()


def split(value):
    high = value.astype(jnp.bfloat16)
    return high, (value - high.astype(jnp.float32)).astype(jnp.bfloat16)


def product(left, right, dims):
    (left_high, left_low), (right_high, right_low) = split(left), split(right)

    def dot(a, b):
        return lax.dot_general(a, b, dims, preferred_element_type=jnp.float32)

    return dot(left_high, right_high) + dot(left_low, right_high) + dot(left_high, right_low)


def turn_plane(tile):
    return jnp.concatenate([tile[:, :LANES].T, tile[:, LANES:].T], 0)


def kernel(sizes, map_ref, states_ref, derivs_ref, gram_ref, rhs_ref, bufs, sems):
    nzh, nzl, ncol, block, states, features = sizes
    nz = nzh * nzl
    far = nz // 2
    width = states + 1
    half = states // nzh
    gram_sum = bufs["gram"]
    slots = gram_sum.shape[0]
    per_core = ncol * block // LANES
    up_slot, down_slot = ring_slots(nz)
    zh, row, col = lax.axis_index("snap"), lax.axis_index("row"), lax.axis_index("col")
    core = lax.rem(row, 2)
    z = zh * nzl + lax.div(row, 2)
    inv_snaps = 1.0 / (nz * 2 * ncol * block)
    own, halves, plane_rows, column = bufs["own"], bufs["halves"], bufs["plane_rows"], bufs["column"]
    land, derivs, feat, turned = bufs["land"], bufs["derivs"], bufs["feat"], bufs["turned"]

    def device(z_to, core_to, col_to):
        return {"snap": lax.div(z_to, nzl), "row": lax.rem(z_to, nzl) * 2 + core_to, "col": col_to}

    def along_z(e):
        return device(lax.rem(z + e + nz, nz), core, col)

    def in_plane(k):
        return device(z, core, lax.rem(col + k, ncol))

    sibling = device(z, 1 - core, col)

    def copy(src, dst, kind, index, to):
        send, recv = sems[kind]
        return pltpu.make_async_remote_copy(
            src_ref=src, dst_ref=dst, send_sem=send.at[index], recv_sem=recv.at[index], device_id=to, device_id_type=MESH
        )

    def each(first, last, act):
        lax.fori_loop(first, last, lambda k, c: (act(k), c)[1], 0)

    load_states = pltpu.make_async_copy(states_ref, bufs["states"], sems["load"][0].at[0])
    load_derivs = pltpu.make_async_copy(derivs_ref, bufs["given"], sems["load"][1].at[0])
    load_states.start()
    load_derivs.start()
    barrier = pltpu.get_barrier_semaphore()

    def greet(to):
        pl.semaphore_signal(barrier, inc=1, device_id=to, device_id_type=MESH)

    greet(sibling)
    each(1, nz, lambda e: greet(along_z(e)))
    each(1, ncol, lambda k: greet(in_plane(k)))

    load_states.wait()
    load_derivs.wait()
    own[...] = jnp.ones(own.shape, jnp.float32)
    own[:, :states] = bufs["states"][...]
    for h in range(nzh):
        halves[h] = jnp.zeros((block, LANES), jnp.float32)
        halves[h, :, :half] = bufs["given"][:, h * half : (h + 1) * half]
    plane_rows[col] = own[...]
    column[0] = halves[zh]

    pl.semaphore_wait(barrier, 1 + (nz - 1) + (ncol - 1))

    def plane_copy(k):
        return copy(own, plane_rows.at[col], "plane", k, in_plane(k))

    def column_copy(e):
        slot = up_slot[e] if e in up_slot else down_slot[nz - e]
        z_to = lax.rem(z + e, nz)
        return copy(halves.at[lax.div(z_to, nzl)], column.at[slot], "column", slot, along_z(e))

    def spread_copy(k):
        return copy(column, derivs.at[0, :, col], "spread", k, in_plane(k))

    def across_copy():
        return copy(derivs.at[0], derivs.at[1], "across", 0, sibling)

    def ring_copies(d, n):
        copies = []
        for slot_of, way, takes in ((up_slot, 1, n < (per_core + 1) // 2), (down_slot, -1, n >= (per_core + 1) // 2)):
            if d < far or (d == far and takes):
                src = slot_of[d - 1] if d > 1 else 0
                dst = slot_of[d] if d < far else up_slot[far]
                copies.append(copy(land.at[src, 0, n], land.at[dst, 0, n], "ring", dst * per_core + n, along_z(way)))
        return copies

    def slots_at(d):
        return [0] if d == 0 else [s[d] for s in (up_slot, down_slot) if d in s]

    def share(slot, n):
        return copy(land.at[slot, 0, n], land.at[slot, 1, n], "share", slot * per_core + n, sibling)

    def pass_on(d, n):
        for c in ring_copies(d, n):
            c.wait_recv()
        for c in ring_copies(d + 1, n):
            c.start()
        for slot in slots_at(d):
            share(slot, n).start()

    def planes_of(d, ns):
        return [(s * 2 + c) * per_core + n for s in slots_at(d) for c in range(2) for n in ns]

    def unfold(d, ns):
        for slot in slots_at(d):
            for n in ns:
                share(slot, n).wait_recv()

        def one(m, carry):
            slot = slots_at(d)[0] + lax.div(m, 2 * len(ns))
            c, n = lax.rem(lax.div(m, len(ns)), 2), lax.rem(m, len(ns)) + ns[0]
            rows = land[slot, c, n][:width]
            plane = (slot * 2 + c) * per_core + n
            feat[plane, :LEAD] = rows[width - LEAD :]
            feat[plane, LEAD : LEAD + width] = rows
            feat[plane, LEAD + width : LEAD + 2 * width] = rows
            feat[plane, LEAD + 2 * width :] = rows[: COPIES - LEAD - 2 * width]
            return carry

        lax.fori_loop(0, len(slots_at(d)) * 2 * len(ns), one, 0)

    def tile_value(place, planes):
        return jnp.concatenate([feature_part(feat, plane, place) for plane in planes], 1)

    def give(p):
        return pltpu.make_async_copy(gram_sum.at[p], gram_ref.at[p], sems["give"][0].at[p])

    def gram(planes, first_time=False, last_time=False, midway=None):
        together = slots // 2

        def one(h, carry):
            if midway is not None:
                pl.when(h == 1)(midway)
            for j in range(together):
                p = h * together + j
                a, b = pair_places(map_ref, p, width)
                term = product(tile_value(a, planes), tile_value(b, planes), NT)
                gram_sum[p] = term if first_time else gram_sum[p] + term
                if last_time:
                    give(p).start()
            return carry

        lax.fori_loop(0, 2, one, 0)

    both = list(range(per_core))
    low, high = both[: (per_core + 1) // 2], both[(per_core + 1) // 2 :]

    def pass_all(d, ns):
        for n in ns:
            pass_on(d, n)

    each(1, ncol, lambda k: plane_copy(k).start())
    for e in range(1, nz):
        column_copy(e).start()
    each(1, ncol, lambda k: plane_copy(k).wait_recv())
    for n in both:
        land[0, 0, n] = turn_plane(plane_rows[...].reshape(per_core, LANES, 2 * LANES)[n])
        for c in ring_copies(1, n):
            c.start()
        share(0, n).start()
    for slot in range(1, nz):
        copy(halves.at[0], column.at[slot], "column", slot, sibling).wait_recv()
    derivs[0, :, col] = column[...]
    each(1, ncol, lambda k: spread_copy(k).start())

    unfold(0, both)
    gram(planes_of(0, both), first_time=True)
    pass_all(1, low)
    for d in range(1, far):
        unfold(d, low)
        gram(planes_of(d, low), midway=functools.partial(pass_all, d, high))
        if high:
            unfold(d, high)
            gram(planes_of(d, high), midway=functools.partial(pass_all, d + 1, low))
        else:
            pass_all(d + 1, low)
    pass_all(far, high)
    each(1, ncol, lambda k: spread_copy(k).wait_recv())
    across_copy().start()
    unfold(far, both)
    gram(planes_of(far, both), last_time=True)

    across_copy().wait_recv()
    rhs_tile = lax.rem(row * ncol + col, CTILES)
    place = tile_place(rhs_tile, width)
    parts = [derivs[c, s].reshape(ncol * block, LANES) for s in range(nz) for c in range(2)]
    total = product(tile_value(place, range(nz * 2 * per_core)), jnp.concatenate(parts, 0), NN)
    total = turn_rows(turned, total, place[0])
    row_at = lax.broadcasted_iota(jnp.int32, total.shape, 0) + rhs_tile * TW
    total = jnp.where(row_at < features, total * inv_snaps, 0.0)
    turned_rhs = jnp.concatenate([total[:LANES].T, total[LANES:].T], 1)
    rhs_ref[0] = turned_rhs[:half]

    each(0, slots, lambda p: give(p).wait())

    each(1, ncol, lambda k: plane_copy(k).wait_send())
    each(1, ncol, lambda k: spread_copy(k).wait_send())
    for e in range(1, nz):
        column_copy(e).wait_send()
    for n in both:
        for d in range(1, far + 1):
            for c in ring_copies(d, n):
                c.wait_send()
        for slot in range(nz):
            share(slot, n).wait_send()
    across_copy().wait_send()


def entry(sizes, names, kinds, *refs):
    refs, flat = refs[: -2 * len(kinds)], refs[-2 * len(kinds) :]
    refs, bufs = refs[: -len(names)], refs[-len(names) :]
    kernel(sizes, *refs, dict(zip(names, bufs)), {k: flat[2 * i : 2 * i + 2] for i, k in enumerate(kinds)})


def local(nzh, nzl, ncol, states, derivatives, tile_map):
    block, width = states.shape
    nz = nzh * nzl
    per_core = ncol * block // LANES
    features = (width + 1) * ((width + 2) // 2)
    slots = tile_map.shape[0]
    shapes = {
        "states": (block, width),
        "given": (block, width),
        "own": (block, 2 * LANES),
        "halves": (nzh, block, LANES),
        "plane_rows": (ncol, block, 2 * LANES),
        "column": (nz, block, LANES),
        "land": (nz, 2, per_core, 2 * LANES, LANES),
        "derivs": (2, nz, ncol, block, LANES),
        "feat": (nz * 2 * per_core, COPIES, LANES),
        "turned": (2, TW + GROUP, LANES),
        "gram": (slots, TW, TW),
    }
    counts = {
        "load": 1,
        "give": slots,
        "plane": ncol,
        "column": nz,
        "spread": ncol,
        "across": 1,
        "ring": nz * per_core,
        "share": nz * per_core,
    }
    out_shape = (
        jax.ShapeDtypeStruct((slots, TW, TW), jnp.float32),
        jax.ShapeDtypeStruct((1, width // nzh, TW), jnp.float32),
    )
    smem, vmem, anywhere = (pl.BlockSpec(memory_space=m) for m in (pltpu.SMEM, pltpu.VMEM, pl.ANY))
    gram_tiles, rhs = pl.pallas_call(
        functools.partial(entry, (nzh, nzl, ncol, block, width, features), tuple(shapes), tuple(counts)),
        out_shape=out_shape,
        in_specs=[smem, anywhere, anywhere],
        out_specs=[anywhere, vmem],
        scratch_shapes=[pltpu.VMEM(shape, jnp.float32) for shape in shapes.values()]
        + [pltpu.SemaphoreType.DMA((count,)) for count in counts.values() for _ in range(2)],
        compiler_params=pltpu.CompilerParams(collective_id=0, has_side_effects=True, vmem_limit_bytes=60 * 2**20),
    )(tile_map.T, states, derivatives)
    gram_tiles, rhs = pl.pallas_call(
        functools.partial(finish, width + 1, features, 1.0 / (nz * 2 * ncol * block)),
        out_shape=out_shape,
        in_specs=[smem, anywhere, anywhere],
        out_specs=[anywhere, anywhere],
        scratch_shapes=[
            pltpu.VMEM((slots, TW, TW), jnp.float32),
            pltpu.VMEM((slots, TW, TW), jnp.float32),
            pltpu.VMEM((2, TW + GROUP, LANES), jnp.float32),
            pltpu.VMEM((1, width // nzh, TW), jnp.float32),
            pltpu.SemaphoreType.DMA((slots,)),
            pltpu.SemaphoreType.DMA((slots,)),
            pltpu.SemaphoreType.DMA((2,)),
        ],
        compiler_params=pltpu.CompilerParams(vmem_limit_bytes=60 * 2**20),
    )(tile_map.T, gram_tiles, rhs)
    return gram_tiles, rhs.transpose(0, 2, 1)


def solution(mesh):
    nzh, rows, ncol = mesh.shape["snap"], mesh.shape["row"], mesh.shape["col"]
    placed = P(("snap", "row", "col"), None)
    return jax.shard_map(
        functools.partial(local, nzh, rows // 2, ncol),
        mesh=mesh,
        in_specs=(placed, placed, placed),
        out_specs=(P(("snap", "row", "col"), None, None), P(("row", "col"), None, "snap")),
        check_vma=False,
    )
```

```python
import functools

import jax
import jax.numpy as jnp
from jax import lax
from jax.experimental import pallas as pl
from jax.experimental.pallas import tpu as pltpu
from jax.sharding import PartitionSpec as P

TW = 256
CTILES = 114
LANES = 128
GROUP = 16
LEAD = GROUP - 1
COPIES = 536
MESH = pl.DeviceIdType.MESH
NT = (((1,), (1,)), ((), ()))
NN = (((1,), (0,)), ((), ()))


def ring_slots(nz):
    up = {d: 2 * d - 1 for d in range(1, nz // 2 + 1)}
    down = {d: 2 * d for d in range(1, (nz + 1) // 2)}
    return up, down


def tile_place(tile, width):
    column = tile * TW
    shift = lax.div(column, width)
    first = column - shift * width
    second = first + shift
    second = jnp.where(second >= width, second - width, second)
    turn = lax.rem(first + GROUP - 1, GROUP)
    wrap = lax.div(width - first + turn, GROUP)
    return turn, wrap, first - turn + LEAD, second - turn + LEAD


def feature_part(feat, plane, place):
    turn, wrap, left, right = place
    rows = lax.broadcasted_iota(jnp.int32, (GROUP, LANES), 0)

    def read(start, size):
        return feat[plane, pl.ds(start, size), :]

    head_left = jnp.where(rows >= turn, read(left, GROUP), read(left + TW, GROUP))
    tail_right = jnp.where(rows >= GROUP * wrap - GROUP + 1, read(right + TW + 2, GROUP), read(right + TW + 1, GROUP))
    head_right = jnp.where(rows >= turn, read(right, GROUP), tail_right)
    body_left = read(left + GROUP, TW - GROUP)
    body_right = [read(right + GROUP * g + jnp.where(g >= wrap, 1, 0), GROUP) for g in range(1, TW // GROUP)]
    return jnp.concatenate([head_left * head_right, body_left * jnp.concatenate(body_right, 0)], 0)


def turn_rows(turned, value, turn):
    for h in range(value.shape[1] // LANES):
        part = value[:, h * LANES : (h + 1) * LANES]
        turned[h, :TW] = part
        turned[h, TW:] = part[:GROUP]
    return jnp.concatenate([turned[h, pl.ds(turn, TW), :] for h in range(value.shape[1] // LANES)], 1)


def pair_places(map_ref, p, width):
    return [tile_place(jnp.maximum(map_ref[q, p], 0), width) for q in range(2)]


def finish(width, features, inv_snaps, map_ref, turned_ref, rhs_in_ref, gram_ref, rhs_ref, taken, given, turned, side, took, gave, rhs_sem):
    slots = taken.shape[0]
    rhs_take = pltpu.make_async_copy(rhs_in_ref, side, rhs_sem.at[0])
    rhs_give = pltpu.make_async_copy(side, rhs_ref, rhs_sem.at[1])
    rhs_take.start()

    def take(p):
        return pltpu.make_async_copy(turned_ref.at[p], taken.at[p], took.at[p])

    def give(p):
        return pltpu.make_async_copy(given.at[p], gram_ref.at[p], gave.at[p])

    for p in range(slots):
        take(p).start()

    def one(p, carry):
        take(p).wait()
        (a, *_), (b, *_) = pair_places(map_ref, p, width)
        total = pltpu.roll(turn_rows(turned, taken[p], a), lax.rem(TW - b, TW), 1)
        row_at = lax.broadcasted_iota(jnp.int32, (TW, TW), 0) + map_ref[0, p] * TW
        col_at = lax.broadcasted_iota(jnp.int32, (TW, TW), 1) + map_ref[1, p] * TW
        live = (map_ref[0, p] >= 0) & (row_at < features) & (col_at < features)
        given[p] = jnp.where(live, total * inv_snaps, 0.0)
        give(p).start()
        return carry

    lax.fori_loop(0, slots, one, 0)
    rhs_take.wait()
    rhs_give.start()
    rhs_give.wait()
    for p in range(slots):
        give(p).wait()


def split(value):
    high = value.astype(jnp.bfloat16)
    return high, (value - high.astype(jnp.float32)).astype(jnp.bfloat16)


def product(left, right, dims):
    (left_high, left_low), (right_high, right_low) = split(left), split(right)

    def dot(a, b):
        return lax.dot_general(a, b, dims, preferred_element_type=jnp.float32)

    rows = left.shape[0]
    both = dot(jnp.concatenate([left_high, left_low], 0), right_high)
    return both[:rows] + both[rows:] + dot(left_high, right_low)


def turn_plane(tile):
    return jnp.concatenate([tile[:, :LANES].T, tile[:, LANES:].T], 0)


def kernel(sizes, map_ref, states_ref, derivs_ref, gram_ref, rhs_ref, bufs, sems):
    nzh, nzl, ncol, block, states, features = sizes
    nz = nzh * nzl
    far = nz // 2
    width = states + 1
    half = states // nzh
    gram_sum = bufs["gram"]
    slots = gram_sum.shape[0]
    per_core = ncol * block // LANES
    up_slot, down_slot = ring_slots(nz)
    zh, row, col = lax.axis_index("snap"), lax.axis_index("row"), lax.axis_index("col")
    core = lax.rem(row, 2)
    z = zh * nzl + lax.div(row, 2)
    inv_snaps = 1.0 / (nz * 2 * ncol * block)
    own, halves, plane_rows, column = bufs["own"], bufs["halves"], bufs["plane_rows"], bufs["column"]
    land, derivs, feat, turned = bufs["land"], bufs["derivs"], bufs["feat"], bufs["turned"]

    def device(z_to, core_to, col_to):
        return {"snap": lax.div(z_to, nzl), "row": lax.rem(z_to, nzl) * 2 + core_to, "col": col_to}

    def along_z(e):
        return device(lax.rem(z + e + nz, nz), core, col)

    def in_plane(k):
        return device(z, core, lax.rem(col + k, ncol))

    sibling = device(z, 1 - core, col)

    def copy(src, dst, kind, index, to):
        send, recv = sems[kind]
        return pltpu.make_async_remote_copy(
            src_ref=src, dst_ref=dst, send_sem=send.at[index], recv_sem=recv.at[index], device_id=to, device_id_type=MESH
        )

    def each(first, last, act):
        lax.fori_loop(first, last, lambda k, c: (act(k), c)[1], 0)

    load_states = pltpu.make_async_copy(states_ref, bufs["states"], sems["load"][0].at[0])
    load_derivs = pltpu.make_async_copy(derivs_ref, bufs["given"], sems["load"][1].at[0])
    load_states.start()
    load_derivs.start()
    barrier = pltpu.get_barrier_semaphore()

    def greet(to):
        pl.semaphore_signal(barrier, inc=1, device_id=to, device_id_type=MESH)

    greet(sibling)
    each(1, nz, lambda e: greet(along_z(e)))
    each(1, ncol, lambda k: greet(in_plane(k)))

    load_states.wait()
    load_derivs.wait()
    own[...] = jnp.ones(own.shape, jnp.float32)
    own[:, :states] = bufs["states"][...]
    for h in range(nzh):
        halves[h] = jnp.zeros((block, LANES), jnp.float32)
        halves[h, :, :half] = bufs["given"][:, h * half : (h + 1) * half]
    plane_rows[col] = own[...]
    column[0] = halves[zh]

    pl.semaphore_wait(barrier, 1 + (nz - 1) + (ncol - 1))

    def plane_copy(k):
        return copy(own, plane_rows.at[col], "plane", k, in_plane(k))

    def column_copy(e):
        slot = up_slot[e] if e in up_slot else down_slot[nz - e]
        z_to = lax.rem(z + e, nz)
        return copy(halves.at[lax.div(z_to, nzl)], column.at[slot], "column", slot, along_z(e))

    def spread_copy(k):
        return copy(column, derivs.at[0, :, col], "spread", k, in_plane(k))

    def across_copy():
        return copy(derivs.at[0], derivs.at[1], "across", 0, sibling)

    def ring_copies(d, n):
        copies = []
        for slot_of, way, takes in ((up_slot, 1, n < (per_core + 1) // 2), (down_slot, -1, n >= (per_core + 1) // 2)):
            if d < far or (d == far and takes):
                src = slot_of[d - 1] if d > 1 else 0
                dst = slot_of[d] if d < far else up_slot[far]
                copies.append(copy(land.at[src, 0, n], land.at[dst, 0, n], "ring", dst * per_core + n, along_z(way)))
        return copies

    def slots_at(d):
        return [0] if d == 0 else [s[d] for s in (up_slot, down_slot) if d in s]

    def share(slot, n):
        return copy(land.at[slot, 0, n], land.at[slot, 1, n], "share", slot * per_core + n, sibling)

    def pass_on(d, n):
        for c in ring_copies(d, n):
            c.wait_recv()
        for c in ring_copies(d + 1, n):
            c.start()
        for slot in slots_at(d):
            share(slot, n).start()

    def planes_of(d, ns):
        return [(s * 2 + c) * per_core + n for s in slots_at(d) for c in range(2) for n in ns]

    def unfold(d, ns):
        for slot in slots_at(d):
            for n in ns:
                share(slot, n).wait_recv()

        def one(m, carry):
            slot = slots_at(d)[0] + lax.div(m, 2 * len(ns))
            c, n = lax.rem(lax.div(m, len(ns)), 2), lax.rem(m, len(ns)) + ns[0]
            rows = land[slot, c, n][:width]
            plane = (slot * 2 + c) * per_core + n
            feat[plane, :LEAD] = rows[width - LEAD :]
            feat[plane, LEAD : LEAD + width] = rows
            feat[plane, LEAD + width : LEAD + 2 * width] = rows
            feat[plane, LEAD + 2 * width :] = rows[: COPIES - LEAD - 2 * width]
            return carry

        lax.fori_loop(0, len(slots_at(d)) * 2 * len(ns), one, 0)

    def tile_value(place, planes):
        return jnp.concatenate([feature_part(feat, plane, place) for plane in planes], 1)

    def give(p):
        return pltpu.make_async_copy(gram_sum.at[p], gram_ref.at[p], sems["give"][0].at[p])

    def gram(planes, first_time=False, last_time=False, midway=None):
        together = slots // 2 if midway is not None else slots

        def one(h, carry):
            if midway is not None:
                pl.when(h == 1)(midway)
            for j in range(together):
                p = h * together + j
                a, b = pair_places(map_ref, p, width)
                term = product(tile_value(a, planes), tile_value(b, planes), NT)
                gram_sum[p] = term if first_time else gram_sum[p] + term
                if last_time:
                    give(p).start()
            return carry

        lax.fori_loop(0, slots // together, one, 0)

    both = list(range(per_core))
    low, high = both[: (per_core + 1) // 2], both[(per_core + 1) // 2 :]

    def pass_all(d, ns):
        for n in ns:
            pass_on(d, n)

    each(1, ncol, lambda k: plane_copy(k).start())
    for e in range(1, nz):
        column_copy(e).start()
    each(1, ncol, lambda k: plane_copy(k).wait_recv())
    for n in both:
        land[0, 0, n] = turn_plane(plane_rows[...].reshape(per_core, LANES, 2 * LANES)[n])
        for c in ring_copies(1, n):
            c.start()
        share(0, n).start()
    for slot in range(1, nz):
        copy(halves.at[0], column.at[slot], "column", slot, sibling).wait_recv()
    derivs[0, :, col] = column[...]
    each(1, ncol, lambda k: spread_copy(k).start())

    unfold(0, both)
    gram(planes_of(0, both), first_time=True)
    pass_all(1, low)
    for d in range(1, far):
        unfold(d, low)
        gram(planes_of(d, low), midway=functools.partial(pass_all, d, high))
        if high:
            unfold(d, high)
            gram(planes_of(d, high), midway=functools.partial(pass_all, d + 1, low))
        else:
            pass_all(d + 1, low)
    pass_all(far, high)
    each(1, ncol, lambda k: spread_copy(k).wait_recv())
    across_copy().start()
    unfold(far, both)
    gram(planes_of(far, both), last_time=True)

    across_copy().wait_recv()
    rhs_tile = lax.rem(row * ncol + col, CTILES)
    place = tile_place(rhs_tile, width)
    parts = [derivs[c, s].reshape(ncol * block, LANES) for s in range(nz) for c in range(2)]
    total = product(tile_value(place, range(nz * 2 * per_core)), jnp.concatenate(parts, 0), NN)
    total = turn_rows(turned, total, place[0])
    row_at = lax.broadcasted_iota(jnp.int32, total.shape, 0) + rhs_tile * TW
    total = jnp.where(row_at < features, total * inv_snaps, 0.0)
    turned_rhs = jnp.concatenate([total[:LANES].T, total[LANES:].T], 1)
    rhs_ref[0] = turned_rhs[:half]

    each(0, slots, lambda p: give(p).wait())

    each(1, ncol, lambda k: plane_copy(k).wait_send())
    each(1, ncol, lambda k: spread_copy(k).wait_send())
    for e in range(1, nz):
        column_copy(e).wait_send()
    for n in both:
        for d in range(1, far + 1):
            for c in ring_copies(d, n):
                c.wait_send()
        for slot in range(nz):
            share(slot, n).wait_send()
    across_copy().wait_send()


def entry(sizes, names, kinds, *refs):
    refs, flat = refs[: -2 * len(kinds)], refs[-2 * len(kinds) :]
    refs, bufs = refs[: -len(names)], refs[-len(names) :]
    kernel(sizes, *refs, dict(zip(names, bufs)), {k: flat[2 * i : 2 * i + 2] for i, k in enumerate(kinds)})


def local(nzh, nzl, ncol, states, derivatives, tile_map):
    block, width = states.shape
    nz = nzh * nzl
    per_core = ncol * block // LANES
    features = (width + 1) * ((width + 2) // 2)
    slots = tile_map.shape[0]
    shapes = {
        "states": (block, width),
        "given": (block, width),
        "own": (block, 2 * LANES),
        "halves": (nzh, block, LANES),
        "plane_rows": (ncol, block, 2 * LANES),
        "column": (nz, block, LANES),
        "land": (nz, 2, per_core, 2 * LANES, LANES),
        "derivs": (2, nz, ncol, block, LANES),
        "feat": (nz * 2 * per_core, COPIES, LANES),
        "turned": (2, TW + GROUP, LANES),
        "gram": (slots, TW, TW),
    }
    counts = {
        "load": 1,
        "give": slots,
        "plane": ncol,
        "column": nz,
        "spread": ncol,
        "across": 1,
        "ring": nz * per_core,
        "share": nz * per_core,
    }
    out_shape = (
        jax.ShapeDtypeStruct((slots, TW, TW), jnp.float32),
        jax.ShapeDtypeStruct((1, width // nzh, TW), jnp.float32),
    )
    smem, vmem, anywhere = (pl.BlockSpec(memory_space=m) for m in (pltpu.SMEM, pltpu.VMEM, pl.ANY))
    gram_tiles, rhs = pl.pallas_call(
        functools.partial(entry, (nzh, nzl, ncol, block, width, features), tuple(shapes), tuple(counts)),
        out_shape=out_shape,
        in_specs=[smem, anywhere, anywhere],
        out_specs=[anywhere, vmem],
        scratch_shapes=[pltpu.VMEM(shape, jnp.float32) for shape in shapes.values()]
        + [pltpu.SemaphoreType.DMA((count,)) for count in counts.values() for _ in range(2)],
        compiler_params=pltpu.CompilerParams(collective_id=0, has_side_effects=True, vmem_limit_bytes=60 * 2**20),
    )(tile_map.T, states, derivatives)
    gram_tiles, rhs = pl.pallas_call(
        functools.partial(finish, width + 1, features, 1.0 / (nz * 2 * ncol * block)),
        out_shape=out_shape,
        in_specs=[smem, anywhere, anywhere],
        out_specs=[anywhere, anywhere],
        scratch_shapes=[
            pltpu.VMEM((slots, TW, TW), jnp.float32),
            pltpu.VMEM((slots, TW, TW), jnp.float32),
            pltpu.VMEM((2, TW + GROUP, LANES), jnp.float32),
            pltpu.VMEM((1, width // nzh, TW), jnp.float32),
            pltpu.SemaphoreType.DMA((slots,)),
            pltpu.SemaphoreType.DMA((slots,)),
            pltpu.SemaphoreType.DMA((2,)),
        ],
        compiler_params=pltpu.CompilerParams(vmem_limit_bytes=60 * 2**20),
    )(tile_map.T, gram_tiles, rhs)
    return gram_tiles, rhs.transpose(0, 2, 1)


def solution(mesh):
    nzh, rows, ncol = mesh.shape["snap"], mesh.shape["row"], mesh.shape["col"]
    placed = P(("snap", "row", "col"), None)
    return jax.shard_map(
        functools.partial(local, nzh, rows // 2, ncol),
        mesh=mesh,
        in_specs=(placed, placed, placed),
        out_specs=(P(("snap", "row", "col"), None, None), P(("row", "col"), None, "snap")),
        check_vma=False,
    )
```
